1024 devices in a mesh: hid: 64 (over x, y), wid: 16 (over z, core).
Axes of the slice: x: 8, y: 8, z: 8, core: 2. Of those that a mesh axis runs over, the one named last changes fastest.
Arguments:
- tokens: bfloat16 [256, 16384], P('hid', 'wid'), may hold values from -6 to 6
- gate_weight: bfloat16 [16384, 26624], P('wid', 'hid'), may hold values from -0.046875 to 0.046875
- up_weight: bfloat16 [16384, 26624], P('wid', 'hid'), may hold values from -0.046875 to 0.046875
- down_weight: bfloat16 [26624, 16384], P('hid', 'wid'), may hold values from -0.0390625 to 0.0390625
Outputs:
- stream: bfloat16 [256, 16384], P('hid', 'wid')
The draws below stay inside these ranges and needn't reach their ends.
All inputs are finite; a program needn't handle non-finite values.
Results may differ from the reference program's by a relative error of at most 0.035.
Values may be sent and summed in bfloat16 or wider, within the bound.
No kernel may reach another device: no remote copies, remote signals or barrier semaphores. Data moves between devices by JAX's collectives and lax.ppermute only.
A program may use at most 32 MiB of HBM per device.

```python
import jax
import jax.numpy as jnp
from jax import lax

D = 16384
FF = 26624
STEPS = 2
ROWS = 256
N_WID = 16


def shard_levels(own_key, shape, shards, low, high):
    factor_of, own = 1.0, jax.random.fold_in(own_key, 6)
    for dim, parts in shards:
        draws = jnp.exp(jax.random.uniform(jax.random.fold_in(own, dim), (parts,), jnp.float32, low / len(shards), high / len(shards)))
        factor_of = factor_of * jnp.repeat(draws, shape[dim] // parts).reshape([-1 if axis == dim else 1 for axis in range(len(shape))])
    return factor_of


def scatter_about(rng, dims, spread, bound, pieces=(), held_as=jnp.bfloat16):
    values = jax.random.normal(rng, dims, jnp.float32) * spread
    if len(pieces) > 0:
        values = shard_levels(rng, dims, pieces, -0.22, 0.18) * values
    return jnp.clip(values, min=-bound, max=bound).astype(held_as)


def setup_inputs(seed: int = 0) -> dict:
    arg_keys = jax.random.split(jax.random.key(seed), 5)
    tokens = scatter_about(arg_keys[0], (ROWS, D), 1.0, 6.0, ((0, 64), (1, 16)))
    gate_weight = scatter_about(arg_keys[1], (D, FF), D ** -0.5, 0.046875, ((0, 16), (1, 64)))
    up_weight = scatter_about(arg_keys[2], (D, FF), D ** -0.5, 0.046875, ((0, 16), (1, 64)))
    down_weight = scatter_about(arg_keys[3], (FF, D), FF ** -0.5, 0.0390625, ((0, 64), (1, 16)))
    return {"tokens": tokens, "gate_weight": gate_weight, "up_weight": up_weight, "down_weight": down_weight}


def reference(tokens, gate_weight, up_weight, down_weight):
    span_cols = D // N_WID
    stream = tokens
    for repeat in range(STEPS):
        def add_group(index, totals):
            offset = (index * span_cols).astype(jnp.int32)
            columns = lax.dynamic_slice_in_dim(stream, offset, span_cols, 1)
            gate_rows = lax.dynamic_slice_in_dim(gate_weight, offset, span_cols, 0)
            up_rows = lax.dynamic_slice_in_dim(up_weight, offset, span_cols, 0)
            gate_part = lax.optimization_barrier(jnp.dot(columns, gate_rows, preferred_element_type=jnp.float32).astype(jnp.bfloat16))
            up_part = lax.optimization_barrier(jnp.dot(columns, up_rows, preferred_element_type=jnp.float32).astype(jnp.bfloat16))
            return (totals[0] + gate_part.astype(jnp.float32), totals[1] + up_part.astype(jnp.float32))

        empty = jnp.zeros((stream.shape[0], gate_weight.shape[1]), jnp.float32)
        gate, up = lax.fori_loop(jnp.int32(0), jnp.int32(N_WID), add_group, (empty, empty))
        hidden = (jax.nn.silu(gate) * up).astype(jnp.bfloat16)
        branch = jnp.dot(hidden, down_weight, preferred_element_type=jnp.float32)
        stream = (stream.astype(jnp.float32) + branch).astype(jnp.bfloat16)
    return stream
```

```python
import jax
import jax.numpy as jnp
from jax import lax
from jax.sharding import PartitionSpec as P

STEPS = 2


def per_device(tokens, gate_weight, up_weight, down_weight):
    n_hid, n_wid = lax.axis_size("hid"), lax.axis_size("wid")
    own, span = tokens.shape
    rows = n_hid * own
    units = gate_weight.shape[1]
    stream = tokens
    for repeat in range(STEPS):
        copies = jnp.broadcast_to(stream[None], (n_hid, own, span))
        shard_rows = lax.all_to_all(copies, "hid", 0, 0, tiled=True).reshape(rows, span)
        gate_part = jnp.dot(shard_rows, gate_weight, preferred_element_type=jnp.float32)
        up_part = jnp.dot(shard_rows, up_weight, preferred_element_type=jnp.float32)
        partial_value = jnp.concatenate(
            [gate_part.astype(jnp.bfloat16), up_part.astype(jnp.bfloat16)], axis=1
        )
        parts = lax.all_to_all(
            partial_value.reshape(n_wid, rows // n_wid, 2 * units), "wid", 0, 0, tiled=True
        )
        totals = jnp.sum(parts.astype(jnp.float32), axis=0)
        own_hidden = (jax.nn.silu(totals[:, :units]) * totals[:, units:]).astype(jnp.bfloat16)
        hidden = lax.all_gather(own_hidden, "wid", axis=0, tiled=True)
        down_part = jnp.dot(hidden, down_weight, preferred_element_type=jnp.float32)
        parts = lax.all_to_all(
            down_part.astype(jnp.bfloat16).reshape(n_hid, own, span), "hid", 0, 0, tiled=True
        )
        branch = jnp.sum(parts.astype(jnp.float32), axis=0)
        stream = (stream.astype(jnp.float32) + branch).astype(jnp.bfloat16)
    return stream


def solution(mesh):
    in_specs = (P("hid", "wid"), P("wid", "hid"), P("wid", "hid"), P("hid", "wid"))
    out_specs = P("hid", "wid")
    return jax.shard_map(
        per_device, mesh=mesh, in_specs=in_specs, out_specs=out_specs, check_vma=False
    )
```

```python
import jax
import jax.numpy as jnp
from jax import lax
from jax.sharding import Mesh, PartitionSpec as P

STEPS = 2
CORES = 2


def product(rows, weight):
    return lax.dot_general(
        rows, weight, (((1,), (1,)), ((), ())), preferred_element_type=jnp.float32
    )


def exchange(parts, axes):
    return lax.all_to_all(parts, axes, 0, 0, tiled=True)


def per_device(tokens, gate_weight, up_weight, down_weight):
    n_hid, n_z = lax.axis_size("hid"), lax.axis_size("z")
    own, span = tokens.shape
    units = gate_weight.shape[1]
    half = own // CORES
    rows = n_hid * half
    core, hid = lax.axis_index("core"), lax.axis_index("hid")
    first = core == 0

    weights = jnp.concatenate([gate_weight.T, up_weight.T, down_weight], axis=0)
    others = lax.ppermute(weights, "core", [(0, 1), (1, 0)])

    copies = jnp.broadcast_to(tokens.reshape(1, CORES, half, span), (n_hid, CORES, half, span))
    gathered = exchange(copies.reshape(n_hid * CORES, half, span), ("hid", "core"))
    gathered = gathered.reshape(n_hid, CORES, half, span)
    low, high = gathered[:, 0], gathered[:, 1]
    gathered = jnp.concatenate(
        [jnp.where(first, low, high), jnp.where(first, high, low)], axis=-1
    )
    stream = lax.dynamic_index_in_dim(gathered, hid, 0, keepdims=False)

    for repeat in range(STEPS):
        if repeat > 0:
            gathered = exchange(
                jnp.broadcast_to(stream[None], (n_hid, half, CORES * span)), "hid"
            )
        shard_rows = gathered.reshape(rows, CORES * span)
        partial_value = product(shard_rows[:, :span], weights[: 2 * units])
        partial_value += product(shard_rows[:, span:], others[: 2 * units])
        parts = exchange(
            partial_value.astype(jnp.bfloat16).reshape(n_z, rows // n_z, 2 * units), "z"
        )
        totals = jnp.sum(parts.astype(jnp.float32), axis=0)
        own_hidden = (jax.nn.silu(totals[:, :units]) * totals[:, units:]).astype(jnp.bfloat16)
        hidden = exchange(
            jnp.broadcast_to(own_hidden[None], (n_z, rows // n_z, units)), "z"
        ).reshape(rows, units)
        here = jnp.dot(hidden, weights[2 * units :], preferred_element_type=jnp.float32)
        there = jnp.dot(hidden, others[2 * units :], preferred_element_type=jnp.float32)
        if repeat < STEPS - 1:
            down_part = jnp.concatenate(
                [here.astype(jnp.bfloat16), there.astype(jnp.bfloat16)], axis=1
            )
            parts = exchange(down_part.reshape(n_hid, half, CORES * span), "hid")
            branch = jnp.sum(parts.astype(jnp.float32), axis=0)
            stream = (stream.astype(jnp.float32) + branch).astype(jnp.bfloat16)

    owner = (jnp.arange(n_hid) == hid)[:, None, None]
    here = here.reshape(n_hid, half, span) + jnp.where(owner, stream[None, :, :span], 0)
    there = there.reshape(n_hid, half, span) + jnp.where(owner, stream[None, :, span:], 0)
    here, there = here.astype(jnp.bfloat16), there.astype(jnp.bfloat16)
    down_part = jnp.stack(
        [jnp.where(first, here, there), jnp.where(first, there, here)], axis=1
    )
    parts = exchange(down_part.reshape(n_hid * CORES, half, span), ("hid", "core"))
    total = jnp.sum(parts.reshape(n_hid, own, span).astype(jnp.float32), axis=0)
    return total.astype(jnp.bfloat16)


def solution(mesh):
    n_hid, n_wid = mesh.devices.shape
    fine = Mesh(mesh.devices.reshape(n_hid, n_wid // CORES, CORES), ("hid", "z", "core"))
    wid = ("z", "core")
    in_specs = (P("hid", wid), P(wid, "hid"), P(wid, "hid"), P("hid", wid))
    out_specs = P("hid", wid)
    return jax.shard_map(
        per_device, mesh=fine, in_specs=in_specs, out_specs=out_specs, check_vma=False
    )
```

```python
import functools

import jax
import jax.numpy as jnp
from jax import lax
from jax.experimental import pallas as pl
from jax.experimental.pallas import tpu as pltpu
from jax.sharding import Mesh, PartitionSpec as P

STEPS = 2
CORES = 2
BLOCKS = 8
F32, BF16 = jnp.float32, jnp.bfloat16
VMEM_BYTES = 16 * 2**20


def dot(a, b):
    return jnp.dot(a, b, preferred_element_type=F32)


def dot_t(a, b):
    return lax.dot_general(a, b, (((1,), (1,)), ((), ())), preferred_element_type=F32)


def kernel_call(body, out_shape, n_in, scalars=False):
    vmem = pl.BlockSpec(memory_space=pltpu.VMEM)
    specs = [pl.BlockSpec(memory_space=pltpu.SMEM)] if scalars else []
    single = not isinstance(out_shape, (list, tuple))
    return pl.pallas_call(
        body,
        out_shape=out_shape,
        in_specs=specs + [vmem] * n_in,
        out_specs=vmem if single else [vmem] * len(out_shape),
        compiler_params=pltpu.CompilerParams(vmem_limit_bytes=VMEM_BYTES),
    )


def store_partial(out, gate, up):
    n, two, units = out.shape
    out[:, : two // 2, :] = gate.astype(BF16).reshape(n, two // 2, units)
    out[:, two // 2 :, :] = up.astype(BF16).reshape(n, two // 2, units)


def first_products(here, there, gate, up, gate_there, up_there, out):
    x, y = here[...], there[...]
    store_partial(
        out,
        dot_t(x, gate[...]) + dot_t(y, gate_there[...]),
        dot_t(x, up[...]) + dot_t(y, up_there[...]),
    )


def block_products(blocks, gate, up, gate_there, up_there, out):
    n_rows, n_cols, rows, cols = blocks.shape
    x = jnp.concatenate(
        [blocks[:, k].reshape(n_rows * rows, cols) for k in range(n_cols)], axis=1
    )
    span = n_cols // 2 * cols
    x, y = x[:, :span], x[:, span:]
    store_partial(
        out,
        dot_t(x, gate[...]) + dot_t(y, gate_there[...]),
        dot_t(x, up[...]) + dot_t(y, up_there[...]),
    )


def activation(parts, out):
    total = parts[0].astype(F32)
    for k in range(1, parts.shape[0]):
        total += parts[k].astype(F32)
    rows = total.shape[0] // 2
    gate, up = total[:rows], total[rows:]
    hidden = (gate / (1.0 + jnp.exp(-gate)) * up).astype(BF16)
    for k in range(out.shape[0]):
        out[k] = hidden


def down_blocks(hidden, down, down_there, out):
    n_rows, n_cols, rows, cols = out.shape
    x = hidden[...].reshape(n_rows * rows, hidden.shape[-1])
    for half, weight in enumerate((down, down_there)):
        for k in range(n_cols // 2):
            value = dot(x, weight[:, k * cols : (k + 1) * cols])
            out[:, half * (n_cols // 2) + k] = value.astype(BF16).reshape(n_rows, rows, cols)


def add_branch(parts, block, out, copies):
    total = parts[0].astype(F32)
    for k in range(1, parts.shape[0]):
        total += parts[k].astype(F32)
    stream = (block[...].astype(F32) + total).astype(BF16)
    out[...] = stream
    for k in range(copies.shape[0]):
        copies[k] = stream


def last_down(place, hidden, down, block, out):
    n, rows, units = hidden.shape
    total, cols = n * rows, block.shape[1]

    def source(width):
        row = lax.broadcasted_iota(jnp.int32, (total, width), 0)
        group, inner = row & ~(CORES * rows - 1), row & (CORES * rows - 1)
        pair = CORES * (rows // BLOCKS)
        owner, within = inner // pair, inner % pair
        return group + within // (pair // CORES) * rows + owner * (pair // CORES) + within % (pair // CORES)

    order = source(total) == lax.broadcasted_iota(jnp.int32, (total, total), 1)
    x = dot(order.astype(F32).astype(BF16), hidden[...].reshape(total, units)).astype(BF16)
    own_rows = source(rows) == lax.broadcasted_iota(jnp.int32, (total, rows), 1) + place[0] * rows
    addend = dot(own_rows.astype(F32).astype(BF16), block[...])
    for k in range(out.shape[1] // cols):
        value = dot(x, down[:, k * cols : (k + 1) * cols])
        value += jnp.where(place[1] == k, addend, 0.0)
        out[:, k * cols : (k + 1) * cols] = value.astype(BF16)


def exchange(parts, axes):
    return lax.all_to_all(parts, axes, 0, 0, tiled=True)


def per_device(tokens, gate, up, down):
    n_hid, n_z = lax.axis_size("hid"), lax.axis_size("z")
    own, span = tokens.shape
    units = gate.shape[1]
    half = own // CORES
    rows = n_hid * half
    chunk = rows // n_z
    block_rows, block_cols = rows // BLOCKS, CORES * span // BLOCKS
    core, hid = lax.axis_index("core"), lax.axis_index("hid")
    first = core == 0
    row_block, col_block = hid // BLOCKS, hid % BLOCKS
    in_own = col_block < BLOCKS // 2
    col_start = col_block % (BLOCKS // 2) * block_cols

    swap = functools.partial(lax.ppermute, axis_name="core", perm=[(0, 1), (1, 0)])
    gate, up = gate.T, up.T
    weights = (gate, up, swap(gate), swap(up))
    down_there = swap(down)

    copies = jnp.broadcast_to(tokens.reshape(1, CORES, half, span), (n_hid, CORES, half, span))
    gathered = exchange(copies.reshape(n_hid * CORES, half, span), ("hid", "core"))
    gathered = gathered.reshape(n_hid, CORES, half, span)
    low, high = gathered[:, 0], gathered[:, 1]
    here = jnp.where(first, low, high).reshape(rows, span)
    there = jnp.where(first, high, low).reshape(rows, span)
    start = (row_block * block_rows, col_start)
    size = (block_rows, block_cols)
    block = jnp.where(
        in_own, lax.dynamic_slice(here, start, size), lax.dynamic_slice(there, start, size)
    )

    partial_shape = jax.ShapeDtypeStruct((n_z, 2 * chunk, units), BF16)
    partial_value = kernel_call(first_products, partial_shape, 6)(here, there, *weights)
    for repeat in range(STEPS):
        last = repeat == STEPS - 1
        parts = exchange(partial_value, "z")
        n_copies = n_z * CORES if last else n_z
        hidden_shape = jax.ShapeDtypeStruct((n_copies, chunk, units), BF16)
        hidden = kernel_call(activation, hidden_shape, 1)(parts)
        hidden = exchange(hidden, ("z", "core") if last else "z")
        if last:
            break
        blocks_shape = jax.ShapeDtypeStruct((BLOCKS, BLOCKS, block_rows, block_cols), BF16)
        down_part = kernel_call(down_blocks, blocks_shape, 3)(hidden, down, down_there)
        parts = exchange(down_part.reshape(n_hid, block_rows, block_cols), "hid")
        block, copies = kernel_call(
            add_branch,
            [
                jax.ShapeDtypeStruct((block_rows, block_cols), BF16),
                jax.ShapeDtypeStruct((n_hid, block_rows, block_cols), BF16),
            ],
            2,
        )(parts, block)
        blocks = exchange(copies, "hid").reshape(blocks_shape.shape)
        partial_value = kernel_call(block_products, partial_shape, 5)(blocks, *weights)

    block = jnp.where(in_own, block, swap(block))
    block_core = jnp.where(in_own, core, 1 - core)
    place = jnp.stack([row_block * CORES + block_core, col_block % (BLOCKS // 2)]).astype(jnp.int32)
    branch = kernel_call(last_down, jax.ShapeDtypeStruct((CORES * rows, span), BF16), 3, True)(
        place, hidden, down, block
    )
    parts = exchange(branch.reshape(n_hid, own, span), "hid")
    return jnp.sum(parts.astype(F32), axis=0).astype(BF16)


def solution(mesh):
    n_hid, n_wid = mesh.devices.shape
    fine = Mesh(mesh.devices.reshape(n_hid, n_wid // CORES, CORES), ("hid", "z", "core"))
    wid = ("z", "core")
    in_specs = (P("hid", wid), P(wid, "hid"), P(wid, "hid"), P("hid", wid))
    out_specs = P("hid", wid)
    return jax.shard_map(
        per_device, mesh=fine, in_specs=in_specs, out_specs=out_specs, check_vma=False
    )
```

```python
import functools

import jax
import jax.numpy as jnp
from jax import lax
from jax.experimental import pallas as pl
from jax.experimental.pallas import tpu as pltpu
from jax.sharding import Mesh, PartitionSpec as P

STEPS = 2
CORES = 2
BLOCKS = 8
F32, BF16 = jnp.float32, jnp.bfloat16
VMEM_BYTES = 16 * 2**20


def dot(a, b):
    return jnp.dot(a, b, preferred_element_type=F32)


def dot_t(a, b):
    return lax.dot_general(a, b, (((1,), (1,)), ((), ())), preferred_element_type=F32)


def kernel_call(body, out_shape, n_in, scalars=False, scratch=()):
    vmem = pl.BlockSpec(memory_space=pltpu.VMEM)
    specs = [pl.BlockSpec(memory_space=pltpu.SMEM)] if scalars else []
    single = not isinstance(out_shape, (list, tuple))
    return pl.pallas_call(
        body,
        out_shape=out_shape,
        in_specs=specs + [vmem] * n_in,
        out_specs=vmem if single else [vmem] * len(out_shape),
        scratch_shapes=scratch,
        compiler_params=pltpu.CompilerParams(vmem_limit_bytes=VMEM_BYTES),
    )


def store_partial(out, gate, up):
    n, two, units = out.shape
    out[:, : two // 2, :] = gate.astype(BF16).reshape(n, two // 2, units)
    out[:, two // 2 :, :] = up.astype(BF16).reshape(n, two // 2, units)


def copy_tokens(tokens, out):
    n, cores, lines, cols = out.shape
    half = tokens.shape[0] // cores
    values = tokens[...].astype(F32)
    for c in range(cores):
        block = jnp.concatenate(
            [
                values[c * half + j : c * half + j + 1, k * cols : (k + 1) * cols]
                for j in range(half)
                for k in range(lines // half)
            ],
            axis=0,
        ).astype(BF16)
        for h in range(n):
            out[h, c] = block


def first_products(place, gathered, gate, up, gate_there, up_there, out, block, stream):
    n_hid, cores, lines, cols = gathered.shape
    n_blocks, rows, _ = stream.shape
    half, parts = rows // n_hid, n_blocks // cores
    owners = min(n_hid, 256 // lines)
    size = owners * lines
    line = lax.broadcasted_iota(jnp.int32, (size, size), 0)
    k, row = line // (owners * half), line % (owners * half)
    source = row // half * lines + row % half * parts + k
    order = (source == lax.broadcasted_iota(jnp.int32, (size, size), 1)).astype(F32).astype(BF16)
    for which in range(cores):
        core = place[0] if which == 0 else 1 - place[0]
        for group in range(n_hid // owners):
            piece = gathered[pl.ds(group * owners, owners), core].reshape(size, cols)
            sorted_piece = dot(order, piece).astype(BF16).reshape(parts, owners * half, cols)
            start = group * owners * half
            stream[which * parts : (which + 1) * parts, start : start + owners * half] = sorted_piece
    size = block.shape[0]
    block[...] = stream[place[2], pl.ds(pl.multiple_of(place[1] * size, size), size), :]
    x, y = (
        jnp.concatenate([stream[which * parts + k] for k in range(parts)], axis=1)
        for which in range(cores)
    )
    store_partial(
        out,
        dot_t(x, gate[...]) + dot_t(y, gate_there[...]),
        dot_t(x, up[...]) + dot_t(y, up_there[...]),
    )


def block_products(blocks, gate, up, gate_there, up_there, out):
    n_rows, n_cols, rows, cols = blocks.shape
    x = jnp.concatenate(
        [blocks[:, k].reshape(n_rows * rows, cols) for k in range(n_cols)], axis=1
    )
    span = n_cols // 2 * cols
    x, y = x[:, :span], x[:, span:]
    store_partial(
        out,
        dot_t(x, gate[...]) + dot_t(y, gate_there[...]),
        dot_t(x, up[...]) + dot_t(y, up_there[...]),
    )


def activation(parts, out):
    total = parts[0].astype(F32)
    for k in range(1, parts.shape[0]):
        total += parts[k].astype(F32)
    rows = total.shape[0] // 2
    gate, up = total[:rows], total[rows:]
    hidden = (gate / (1.0 + jnp.exp(-gate)) * up).astype(BF16)
    for k in range(out.shape[0]):
        out[k] = hidden


def down_blocks(hidden, down, down_there, out):
    n_rows, n_cols, rows, cols = out.shape
    x = hidden[...].reshape(n_rows * rows, hidden.shape[-1])
    for half, weight in enumerate((down, down_there)):
        for k in range(n_cols // 2):
            value = dot(x, weight[:, k * cols : (k + 1) * cols])
            out[:, half * (n_cols // 2) + k] = value.astype(BF16).reshape(n_rows, rows, cols)


def add_branch(parts, block, out, copies):
    total = parts[0].astype(F32)
    for k in range(1, parts.shape[0]):
        total += parts[k].astype(F32)
    stream = (block[...].astype(F32) + total).astype(BF16)
    out[...] = stream
    for k in range(copies.shape[0]):
        copies[k] = stream


def last_down(place, hidden, down, block, out):
    n, rows, units = hidden.shape
    total, cols = n * rows, block.shape[1]

    def source(width):
        row = lax.broadcasted_iota(jnp.int32, (total, width), 0)
        group, inner = row & ~(CORES * rows - 1), row & (CORES * rows - 1)
        pair = CORES * (rows // BLOCKS)
        owner, within = inner // pair, inner % pair
        return group + within // (pair // CORES) * rows + owner * (pair // CORES) + within % (pair // CORES)

    order = source(total) == lax.broadcasted_iota(jnp.int32, (total, total), 1)
    x = dot(order.astype(F32).astype(BF16), hidden[...].reshape(total, units)).astype(BF16)
    own_rows = source(rows) == lax.broadcasted_iota(jnp.int32, (total, rows), 1) + place[0] * rows
    addend = dot(own_rows.astype(F32).astype(BF16), block[...])
    for k in range(out.shape[1] // cols):
        value = dot(x, down[:, k * cols : (k + 1) * cols])
        value += jnp.where(place[1] == k, addend, 0.0)
        out[:, k * cols : (k + 1) * cols] = value.astype(BF16)


def exchange(parts, axes):
    return lax.all_to_all(parts, axes, 0, 0, tiled=True)


def per_device(tokens, gate, up, down):
    n_hid, n_z = lax.axis_size("hid"), lax.axis_size("z")
    own, span = tokens.shape
    units = gate.shape[1]
    half = own // CORES
    rows = n_hid * half
    chunk = rows // n_z
    block_rows, block_cols = rows // BLOCKS, CORES * span // BLOCKS
    core, hid = lax.axis_index("core"), lax.axis_index("hid")
    row_block, col_block = hid // BLOCKS, hid % BLOCKS
    in_own = col_block < BLOCKS // 2

    swap = functools.partial(lax.ppermute, axis_name="core", perm=[(0, 1), (1, 0)])
    gate, up = gate.T, up.T
    weights = (gate, up, swap(gate), swap(up))
    down_there = swap(down)

    lines = half * span // block_cols
    copies_shape = jax.ShapeDtypeStruct((n_hid, CORES, lines, block_cols), BF16)
    copies = kernel_call(copy_tokens, copies_shape, 1)(tokens)
    gathered = exchange(copies.reshape(n_hid * CORES, lines, block_cols), ("hid", "core"))
    partial_shape = jax.ShapeDtypeStruct((n_z, 2 * chunk, units), BF16)
    partial_value, block = kernel_call(
        first_products,
        [partial_shape, jax.ShapeDtypeStruct((block_rows, block_cols), BF16)],
        5,
        True,
        [pltpu.VMEM((BLOCKS, rows, block_cols), BF16)],
    )(
        jnp.stack([core, row_block, col_block]).astype(jnp.int32),
        gathered.reshape(copies_shape.shape),
        *weights,
    )
    partial_value, down_there = lax.optimization_barrier((partial_value, down_there))
    for repeat in range(STEPS):
        last = repeat == STEPS - 1
        parts = exchange(partial_value, "z")
        n_copies = n_z * CORES if last else n_z
        hidden_shape = jax.ShapeDtypeStruct((n_copies, chunk, units), BF16)
        hidden = kernel_call(activation, hidden_shape, 1)(parts)
        hidden = exchange(hidden, ("z", "core") if last else "z")
        if last:
            break
        blocks_shape = jax.ShapeDtypeStruct((BLOCKS, BLOCKS, block_rows, block_cols), BF16)
        down_part = kernel_call(down_blocks, blocks_shape, 3)(hidden, down, down_there)
        parts = exchange(down_part.reshape(n_hid, block_rows, block_cols), "hid")
        block, copies = kernel_call(
            add_branch,
            [
                jax.ShapeDtypeStruct((block_rows, block_cols), BF16),
                jax.ShapeDtypeStruct((n_hid, block_rows, block_cols), BF16),
            ],
            2,
        )(parts, block)
        blocks = exchange(copies, "hid").reshape(blocks_shape.shape)
        partial_value = kernel_call(block_products, partial_shape, 5)(blocks, *weights)

    block = jnp.where(in_own, block, swap(block))
    block_core = jnp.where(in_own, core, 1 - core)
    place = jnp.stack([row_block * CORES + block_core, col_block % (BLOCKS // 2)]).astype(jnp.int32)
    branch = kernel_call(last_down, jax.ShapeDtypeStruct((CORES * rows, span), BF16), 3, True)(
        place, hidden, down, block
    )
    parts = exchange(branch.reshape(n_hid, own, span), "hid")
    return jnp.sum(parts.astype(F32), axis=0).astype(BF16)


def solution(mesh):
    n_hid, n_wid = mesh.devices.shape
    fine = Mesh(mesh.devices.reshape(n_hid, n_wid // CORES, CORES), ("hid", "z", "core"))
    wid = ("z", "core")
    in_specs = (P("hid", wid), P(wid, "hid"), P(wid, "hid"), P("hid", wid))
    out_specs = P("hid", wid)
    return jax.shard_map(
        per_device, mesh=fine, in_specs=in_specs, out_specs=out_specs, check_vma=False
    )
```

```python
import functools

import jax
import jax.numpy as jnp
from jax import lax
from jax.experimental import pallas as pl
from jax.experimental.pallas import tpu as pltpu
from jax.sharding import Mesh, PartitionSpec as P

STEPS = 2
CORES = 2
BLOCKS = 8
F32, BF16 = jnp.float32, jnp.bfloat16
VMEM_BYTES = 8 * 2**20
FIRST_VMEM_BYTES = 60 * 2**20


def dot(a, b):
    return jnp.dot(a, b, preferred_element_type=F32)


def dot_t(a, b):
    return lax.dot_general(a, b, (((1,), (1,)), ((), ())), preferred_element_type=F32)


def kernel_call(body, out_shape, n_in, scalars=0, far=0, scratch=(), limit=VMEM_BYTES):
    vmem = pl.BlockSpec(memory_space=pltpu.VMEM)
    specs = [pl.BlockSpec(memory_space=pltpu.SMEM)] * scalars + [pl.BlockSpec(memory_space=pl.ANY)] * far
    single = not isinstance(out_shape, (list, tuple))
    return pl.pallas_call(
        body,
        out_shape=out_shape,
        in_specs=specs + [vmem] * n_in,
        out_specs=vmem if single else [vmem] * len(out_shape),
        scratch_shapes=scratch,
        compiler_params=pltpu.CompilerParams(vmem_limit_bytes=limit),
    )


def store_partial(out, gate, up):
    n, two, units = out.shape
    out[:, : two // 2, :] = gate.astype(BF16).reshape(n, two // 2, units)
    out[:, two // 2 :, :] = up.astype(BF16).reshape(n, two // 2, units)


def copy_tokens(tokens, out):
    n, cores, lines, cols = out.shape
    half = tokens.shape[0] // cores
    values = tokens[...].astype(F32)
    for c in range(cores):
        block = jnp.concatenate(
            [
                values[c * half + j : c * half + j + 1, k * cols : (k + 1) * cols]
                for j in range(half)
                for k in range(lines // half)
            ],
            axis=0,
        ).astype(BF16)
        for h in range(n):
            out[h, c] = block


def first_products(
    place, gathered_far, gate_far, up_far, gate_there_far, up_there_far, out, block,
    stream, gathered, gate, up, gate_there, up_there, sems,
):
    pairs = (
        (gathered_far, gathered),
        (gate_there_far, gate_there),
        (up_there_far, up_there),
        (gate_far, gate),
        (up_far, up),
    )
    fetches = [pltpu.make_async_copy(*pair, sems.at[i]) for i, pair in enumerate(pairs)]
    for fetch in fetches:
        fetch.start()
    fetches[0].wait()
    n_hid, cores, lines, cols = gathered.shape
    n_blocks, rows, _ = stream.shape
    half, parts = rows // n_hid, n_blocks // cores
    owners = min(n_hid, 256 // lines)
    size = owners * lines
    line = lax.broadcasted_iota(jnp.int32, (size, size), 0)
    k, row = line // (owners * half), line % (owners * half)
    source = row // half * lines + row % half * parts + k
    order = (source == lax.broadcasted_iota(jnp.int32, (size, size), 1)).astype(F32).astype(BF16)
    for which in range(cores):
        core = place[0] if which == 0 else 1 - place[0]
        for group in range(n_hid // owners):
            piece = gathered[pl.ds(group * owners, owners), core].reshape(size, cols)
            sorted_piece = dot(order, piece).astype(BF16).reshape(parts, owners * half, cols)
            start = group * owners * half
            stream[which * parts : (which + 1) * parts, start : start + owners * half] = sorted_piece
    size = block.shape[0]
    block[...] = stream[place[2], pl.ds(pl.multiple_of(place[1] * size, size), size), :]
    x, y = (
        jnp.concatenate([stream[which * parts + k] for k in range(parts)], axis=1)
        for which in range(cores)
    )
    fetches[1].wait()
    gate_sum = dot_t(y, gate_there[...])
    fetches[2].wait()
    up_sum = dot_t(y, up_there[...])
    fetches[3].wait()
    gate_sum += dot_t(x, gate[...])
    fetches[4].wait()
    up_sum += dot_t(x, up[...])
    store_partial(out, gate_sum, up_sum)


def block_products(blocks, gate, up, gate_there, up_there, out):
    n_rows, n_cols, rows, cols = blocks.shape
    x, y = (
        jnp.concatenate([blocks[:, k].reshape(n_rows * rows, cols) for k in part], axis=1)
        for part in (range(n_cols // 2), range(n_cols // 2, n_cols))
    )
    store_partial(
        out,
        dot_t(x, gate[...]) + dot_t(y, gate_there[...]),
        dot_t(x, up[...]) + dot_t(y, up_there[...]),
    )


def activation(parts, out):
    total = parts[0].astype(F32)
    for k in range(1, parts.shape[0]):
        total += parts[k].astype(F32)
    rows = total.shape[0] // 2
    gate, up = total[:rows], total[rows:]
    hidden = (gate / (1.0 + jnp.exp(-gate)) * up).astype(BF16)
    for k in range(out.shape[0]):
        out[k] = hidden


def down_blocks(there_far, hidden, down, out, down_there, sems):
    fetch = pltpu.make_async_copy(there_far, down_there, sems.at[0])
    fetch.start()
    n_rows, n_cols, rows, cols = out.shape
    x = hidden[...].reshape(n_rows * rows, hidden.shape[-1])
    for half, weight in enumerate((down, down_there)):
        if half == 1:
            fetch.wait()
        for k in range(n_cols // 2):
            value = dot(x, weight[:, k * cols : (k + 1) * cols])
            out[:, half * (n_cols // 2) + k] = value.astype(BF16).reshape(n_rows, rows, cols)


def add_branch(parts, block, out, copies):
    total = parts[0].astype(F32)
    for k in range(1, parts.shape[0]):
        total += parts[k].astype(F32)
    stream = (block[...].astype(F32) + total).astype(BF16)
    out[...] = stream
    for k in range(copies.shape[0]):
        copies[k] = stream


def last_down(place, hidden, down, block, out):
    n, rows, units = hidden.shape
    total, cols = n * rows, block.shape[1]

    def source(width):
        row = lax.broadcasted_iota(jnp.int32, (total, width), 0)
        group, inner = row & ~(CORES * rows - 1), row & (CORES * rows - 1)
        pair = CORES * (rows // BLOCKS)
        owner, within = inner // pair, inner % pair
        return group + within // (pair // CORES) * rows + owner * (pair // CORES) + within % (pair // CORES)

    order = source(total) == lax.broadcasted_iota(jnp.int32, (total, total), 1)
    x = dot(order.astype(F32).astype(BF16), hidden[...].reshape(total, units)).astype(BF16)
    own_rows = source(rows) == lax.broadcasted_iota(jnp.int32, (total, rows), 1) + place[0] * rows
    addend = dot(own_rows.astype(F32).astype(BF16), block[...])
    n_blocks, own = down.shape[1] // cols, out.shape[2] // (down.shape[1] // cols)
    values, rolled = [], []
    for k in range(n_blocks):
        value = dot(x, down[:, k * cols : (k + 1) * cols])
        value += jnp.where(place[1] == k, addend, 0.0)
        values.append(value.reshape(total // (2 * own), 2 * own, cols))
        rolled.append(pltpu.roll(values[-1], own, 1))
    upper = lax.broadcasted_iota(jnp.int32, values[0].shape, 1) < own
    for k in range(0, n_blocks, 2):
        lines = slice(k * own, (k + 2) * own)
        out[:, 0, lines] = jnp.where(upper, values[k], rolled[k + 1]).astype(BF16)
        out[:, 1, lines] = jnp.where(upper, rolled[k], values[k + 1]).astype(BF16)


def final_sum(parts, out):
    total = parts[0].astype(F32)
    for k in range(1, parts.shape[0]):
        total += parts[k].astype(F32)
    own, cols = out.shape[0], total.shape[1]
    for k in range(out.shape[1] // cols):
        out[:, k * cols : (k + 1) * cols] = total[k * own : (k + 1) * own].astype(BF16)


def exchange(parts, axes):
    return lax.all_to_all(parts, axes, 0, 0, tiled=True)


def per_device(tokens, gate, up, down):
    n_hid, n_z = lax.axis_size("hid"), lax.axis_size("z")
    own, span = tokens.shape
    units = gate.shape[1]
    half = own // CORES
    rows = n_hid * half
    chunk = rows // n_z
    block_rows, block_cols = rows // BLOCKS, CORES * span // BLOCKS
    core, hid = lax.axis_index("core"), lax.axis_index("hid")
    row_block, col_block = hid // BLOCKS, hid % BLOCKS
    in_own = col_block < BLOCKS // 2

    swap = functools.partial(lax.ppermute, axis_name="core", perm=[(0, 1), (1, 0)])
    gate, up = gate.T, up.T
    weights = (gate, up, swap(gate), swap(up))
    down_there = swap(down)

    lines = half * span // block_cols
    copies_shape = jax.ShapeDtypeStruct((n_hid, CORES, lines, block_cols), BF16)
    copies = kernel_call(copy_tokens, copies_shape, 1)(tokens)
    gathered = exchange(copies.reshape(n_hid * CORES, lines, block_cols), ("hid", "core"))
    partial_shape = jax.ShapeDtypeStruct((n_z, 2 * chunk, units), BF16)
    partial_value, block = kernel_call(
        first_products,
        [partial_shape, jax.ShapeDtypeStruct((block_rows, block_cols), BF16)],
        0,
        scalars=1,
        far=5,
        scratch=[
            pltpu.VMEM((BLOCKS, rows, block_cols), BF16),
            pltpu.VMEM(copies_shape.shape, BF16),
            *(pltpu.VMEM(gate.shape, BF16) for _ in weights),
            pltpu.SemaphoreType.DMA((5,)),
        ],
        limit=FIRST_VMEM_BYTES,
    )(
        jnp.stack([core, row_block, col_block]).astype(jnp.int32),
        gathered.reshape(copies_shape.shape),
        *weights,
    )
    partial_value, down_there = lax.optimization_barrier((partial_value, down_there))
    for repeat in range(STEPS):
        last = repeat == STEPS - 1
        parts = exchange(partial_value, "z")
        n_copies = n_z * CORES if last else n_z
        hidden_shape = jax.ShapeDtypeStruct((n_copies, chunk, units), BF16)
        hidden = kernel_call(activation, hidden_shape, 1)(parts)
        hidden = exchange(hidden, ("z", "core") if last else "z")
        if last:
            break
        blocks_shape = jax.ShapeDtypeStruct((BLOCKS, BLOCKS, block_rows, block_cols), BF16)
        down_part = kernel_call(
            down_blocks,
            blocks_shape,
            2,
            far=1,
            scratch=[pltpu.VMEM(down.shape, BF16), pltpu.SemaphoreType.DMA((1,))],
        )(down_there, hidden, down)
        parts = exchange(down_part.reshape(n_hid, block_rows, block_cols), "hid")
        block, copies = kernel_call(
            add_branch,
            [
                jax.ShapeDtypeStruct((block_rows, block_cols), BF16),
                jax.ShapeDtypeStruct((n_hid, block_rows, block_cols), BF16),
            ],
            2,
        )(parts, block)
        blocks = exchange(copies, "hid").reshape(blocks_shape.shape)
        partial_value = kernel_call(block_products, partial_shape, 5)(blocks, *weights)

    block = jnp.where(in_own, block, swap(block))
    block_core = jnp.where(in_own, core, 1 - core)
    place = jnp.stack([row_block * CORES + block_core, col_block % (BLOCKS // 2)]).astype(jnp.int32)
    n_lines = own * span // block_cols
    branch_shape = jax.ShapeDtypeStruct((n_hid // 2, 2, n_lines, block_cols), BF16)
    branch = kernel_call(last_down, branch_shape, 3, scalars=1)(place, hidden, down, block)
    parts = exchange(branch.reshape(n_hid, n_lines, block_cols), "hid")
    return kernel_call(final_sum, jax.ShapeDtypeStruct((own, span), BF16), 1)(parts)


def solution(mesh):
    n_hid, n_wid = mesh.devices.shape
    fine = Mesh(mesh.devices.reshape(n_hid, n_wid // CORES, CORES), ("hid", "z", "core"))
    wid = ("z", "core")
    in_specs = (P("hid", wid), P(wid, "hid"), P(wid, "hid"), P("hid", wid))
    out_specs = P("hid", wid)
    return jax.shard_map(
        per_device, mesh=fine, in_specs=in_specs, out_specs=out_specs, check_vma=False
    )
```

```python
import functools

import jax
import jax.numpy as jnp
from jax import lax
from jax.experimental import pallas as pl
from jax.experimental.pallas import tpu as pltpu
from jax.sharding import Mesh, PartitionSpec as P

STEPS = 2
FETCHES = 2
CORES = 2
BLOCKS = 8
F32, BF16 = jnp.float32, jnp.bfloat16
VMEM_BYTES = 8 * 2**20
FIRST_VMEM_BYTES = 53 * 2**20


def dot(a, b):
    return jnp.dot(a, b, preferred_element_type=F32)


def dot_t(a, b):
    return lax.dot_general(a, b, (((1,), (1,)), ((), ())), preferred_element_type=F32)


def kernel_call(body, out_shape, n_in, scalars=0, far=0, scratch=(), limit=VMEM_BYTES):
    vmem = pl.BlockSpec(memory_space=pltpu.VMEM)
    specs = [pl.BlockSpec(memory_space=pltpu.SMEM)] * scalars + [pl.BlockSpec(memory_space=pl.ANY)] * far
    single = not isinstance(out_shape, (list, tuple))
    return pl.pallas_call(
        body,
        out_shape=out_shape,
        in_specs=specs + [vmem] * n_in,
        out_specs=vmem if single else [vmem] * len(out_shape),
        scratch_shapes=scratch,
        compiler_params=pltpu.CompilerParams(vmem_limit_bytes=limit),
    )


def store_partial(out, gate, up):
    n, two, units = out.shape
    out[:, : two // 2, :] = gate.astype(BF16).reshape(n, two // 2, units)
    out[:, two // 2 :, :] = up.astype(BF16).reshape(n, two // 2, units)


def copy_tokens(tokens, out):
    n, cores, lines, cols = out.shape
    half = tokens.shape[0] // cores
    values = tokens[...].astype(F32)
    for c in range(cores):
        block = jnp.concatenate(
            [
                values[c * half + j : c * half + j + 1, k * cols : (k + 1) * cols]
                for j in range(half)
                for k in range(lines // half)
            ],
            axis=0,
        ).astype(BF16)
        for h in range(n):
            out[h, c] = block


def first_products(
    place, gate_far, up_far, gate_there_far, up_there_far, gathered, out, block,
    stream, gate, up, gate_there, up_there, sems,
):
    pairs = (
        (gate_there_far, gate_there),
        (up_there_far, up_there),
        (gate_far, gate),
        (up_far, up),
    )
    part = gate.shape[0] // FETCHES
    fetches = [
        [
            pltpu.make_async_copy(
                far.at[pl.ds(k * part, part)], near.at[pl.ds(k * part, part)], sems.at[i, k]
            )
            for k in range(FETCHES)
        ]
        for i, (far, near) in enumerate(pairs)
    ]
    for group in fetches:
        for fetch in group:
            fetch.start()

    def arrive(i):
        for fetch in fetches[i]:
            fetch.wait()

    n_hid, cores, lines, cols = gathered.shape
    n_blocks, rows, _ = stream.shape
    half, parts = rows // n_hid, n_blocks // cores
    owners = min(n_hid, 256 // lines)
    size = owners * lines
    line = lax.broadcasted_iota(jnp.int32, (size, size), 0)
    k, row = line // (owners * half), line % (owners * half)
    source = row // half * lines + row % half * parts + k
    order = (source == lax.broadcasted_iota(jnp.int32, (size, size), 1)).astype(F32).astype(BF16)
    for which in range(cores):
        core = place[0] if which == 0 else 1 - place[0]
        for group in range(n_hid // owners):
            piece = gathered[pl.ds(group * owners, owners), core].reshape(size, cols)
            sorted_piece = dot(order, piece).astype(BF16).reshape(parts, owners * half, cols)
            start = group * owners * half
            stream[which * parts : (which + 1) * parts, start : start + owners * half] = sorted_piece
    size = block.shape[0]
    block[...] = stream[place[2], pl.ds(pl.multiple_of(place[1] * size, size), size), :]
    x, y = (
        jnp.concatenate([stream[which * parts + k] for k in range(parts)], axis=1)
        for which in range(cores)
    )
    arrive(0)
    gate_sum = dot_t(y, gate_there[...])
    arrive(1)
    up_sum = dot_t(y, up_there[...])
    arrive(2)
    gate_sum += dot_t(x, gate[...])
    arrive(3)
    up_sum += dot_t(x, up[...])
    store_partial(out, gate_sum, up_sum)


def block_products(blocks, gate, up, gate_there, up_there, out):
    n_rows, n_cols, rows, cols = blocks.shape
    x, y = (
        jnp.concatenate([blocks[:, k].reshape(n_rows * rows, cols) for k in part], axis=1)
        for part in (range(n_cols // 2), range(n_cols // 2, n_cols))
    )
    store_partial(
        out,
        dot_t(x, gate[...]) + dot_t(y, gate_there[...]),
        dot_t(x, up[...]) + dot_t(y, up_there[...]),
    )


def activation(parts, out):
    total = parts[0].astype(F32)
    for k in range(1, parts.shape[0]):
        total += parts[k].astype(F32)
    rows = total.shape[0] // 2
    gate, up = total[:rows], total[rows:]
    hidden = (gate / (1.0 + jnp.exp(-gate)) * up).astype(BF16)
    for k in range(out.shape[0]):
        out[k] = hidden


def down_blocks(there_far, hidden, down, out, down_there, sems):
    fetch = pltpu.make_async_copy(there_far, down_there, sems.at[0])
    fetch.start()
    n_rows, n_cols, rows, cols = out.shape
    x = hidden[...].reshape(n_rows * rows, hidden.shape[-1])
    for half, weight in enumerate((down, down_there)):
        if half == 1:
            fetch.wait()
        for k in range(n_cols // 2):
            value = dot(x, weight[:, k * cols : (k + 1) * cols])
            out[:, half * (n_cols // 2) + k] = value.astype(BF16).reshape(n_rows, rows, cols)


def add_branch(parts, block, out, copies):
    total = parts[0].astype(F32)
    for k in range(1, parts.shape[0]):
        total += parts[k].astype(F32)
    stream = (block[...].astype(F32) + total).astype(BF16)
    out[...] = stream
    for k in range(copies.shape[0]):
        copies[k] = stream


def last_down(place, hidden, down, block, out):
    n, rows, units = hidden.shape
    total, cols = n * rows, block.shape[1]

    def source(width):
        row = lax.broadcasted_iota(jnp.int32, (total, width), 0)
        group, inner = row & ~(CORES * rows - 1), row & (CORES * rows - 1)
        pair = CORES * (rows // BLOCKS)
        owner, within = inner // pair, inner % pair
        return group + within // (pair // CORES) * rows + owner * (pair // CORES) + within % (pair // CORES)

    order = source(total) == lax.broadcasted_iota(jnp.int32, (total, total), 1)
    x = dot(order.astype(F32).astype(BF16), hidden[...].reshape(total, units)).astype(BF16)
    own_rows = source(rows) == lax.broadcasted_iota(jnp.int32, (total, rows), 1) + place[0] * rows
    addend = dot(own_rows.astype(F32).astype(BF16), block[...])
    n_blocks, own = down.shape[1] // cols, out.shape[2] // (down.shape[1] // cols)
    values, rolled = [], []
    for k in range(n_blocks):
        value = dot(x, down[:, k * cols : (k + 1) * cols])
        value += jnp.where(place[1] == k, addend, 0.0)
        values.append(value.reshape(total // (2 * own), 2 * own, cols))
        rolled.append(pltpu.roll(values[-1], own, 1))
    upper = lax.broadcasted_iota(jnp.int32, values[0].shape, 1) < own
    for k in range(0, n_blocks, 2):
        lines = slice(k * own, (k + 2) * own)
        out[:, 0, lines] = jnp.where(upper, values[k], rolled[k + 1]).astype(BF16)
        out[:, 1, lines] = jnp.where(upper, rolled[k], values[k + 1]).astype(BF16)


def final_sum(parts, out):
    total = parts[0].astype(F32)
    for k in range(1, parts.shape[0]):
        total += parts[k].astype(F32)
    own, cols = out.shape[0], total.shape[1]
    for k in range(out.shape[1] // cols):
        out[:, k * cols : (k + 1) * cols] = total[k * own : (k + 1) * own].astype(BF16)


def exchange(parts, axes):
    return lax.all_to_all(parts, axes, 0, 0, tiled=True)


def per_device(tokens, gate, up, down):
    n_hid, n_z = lax.axis_size("hid"), lax.axis_size("z")
    own, span = tokens.shape
    units = gate.shape[1]
    half = own // CORES
    rows = n_hid * half
    chunk = rows // n_z
    block_rows, block_cols = rows // BLOCKS, CORES * span // BLOCKS
    core, hid = lax.axis_index("core"), lax.axis_index("hid")
    row_block, col_block = hid // BLOCKS, hid % BLOCKS
    in_own = col_block < BLOCKS // 2

    swap = functools.partial(lax.ppermute, axis_name="core", perm=[(0, 1), (1, 0)])
    gate, up = gate.T, up.T
    weights = (gate, up, swap(gate), swap(up))
    down_there = swap(down)

    lines = half * span // block_cols
    copies_shape = jax.ShapeDtypeStruct((n_hid, CORES, lines, block_cols), BF16)
    copies = kernel_call(copy_tokens, copies_shape, 1)(tokens)
    gathered = exchange(copies.reshape(n_hid * CORES, lines, block_cols), ("hid", "core"))
    partial_shape = jax.ShapeDtypeStruct((n_z, 2 * chunk, units), BF16)
    partial_value, block = kernel_call(
        first_products,
        [partial_shape, jax.ShapeDtypeStruct((block_rows, block_cols), BF16)],
        1,
        scalars=1,
        far=4,
        scratch=[
            pltpu.VMEM((BLOCKS, rows, block_cols), BF16),
            *(pltpu.VMEM(gate.shape, BF16) for _ in weights),
            pltpu.SemaphoreType.DMA((4, FETCHES)),
        ],
        limit=FIRST_VMEM_BYTES,
    )(
        jnp.stack([core, row_block, col_block]).astype(jnp.int32),
        *weights,
        gathered.reshape(copies_shape.shape),
    )
    partial_value, down_there = lax.optimization_barrier((partial_value, down_there))
    for repeat in range(STEPS):
        last = repeat == STEPS - 1
        parts = exchange(partial_value, "z")
        n_copies = n_z * CORES if last else n_z
        hidden_shape = jax.ShapeDtypeStruct((n_copies, chunk, units), BF16)
        hidden = kernel_call(activation, hidden_shape, 1)(parts)
        hidden = exchange(hidden, ("z", "core") if last else "z")
        if last:
            break
        blocks_shape = jax.ShapeDtypeStruct((BLOCKS, BLOCKS, block_rows, block_cols), BF16)
        down_part = kernel_call(
            down_blocks,
            blocks_shape,
            2,
            far=1,
            scratch=[pltpu.VMEM(down.shape, BF16), pltpu.SemaphoreType.DMA((1,))],
        )(down_there, hidden, down)
        parts = exchange(down_part.reshape(n_hid, block_rows, block_cols), "hid")
        block, copies = kernel_call(
            add_branch,
            [
                jax.ShapeDtypeStruct((block_rows, block_cols), BF16),
                jax.ShapeDtypeStruct((n_hid, block_rows, block_cols), BF16),
            ],
            2,
        )(parts, block)
        blocks = exchange(copies, "hid").reshape(blocks_shape.shape)
        partial_value = kernel_call(block_products, partial_shape, 5)(blocks, *weights)

    block = jnp.where(in_own, block, swap(block))
    block_core = jnp.where(in_own, core, 1 - core)
    place = jnp.stack([row_block * CORES + block_core, col_block % (BLOCKS // 2)]).astype(jnp.int32)
    n_lines = own * span // block_cols
    branch_shape = jax.ShapeDtypeStruct((n_hid // 2, 2, n_lines, block_cols), BF16)
    branch = kernel_call(last_down, branch_shape, 3, scalars=1)(place, hidden, down, block)
    parts = exchange(branch.reshape(n_hid, n_lines, block_cols), "hid")
    return kernel_call(final_sum, jax.ShapeDtypeStruct((own, span), BF16), 1)(parts)


def solution(mesh):
    n_hid, n_wid = mesh.devices.shape
    fine = Mesh(mesh.devices.reshape(n_hid, n_wid // CORES, CORES), ("hid", "z", "core"))
    wid = ("z", "core")
    in_specs = (P("hid", wid), P(wid, "hid"), P(wid, "hid"), P("hid", wid))
    out_specs = P("hid", wid)
    return jax.shard_map(
        per_device, mesh=fine, in_specs=in_specs, out_specs=out_specs, check_vma=False
    )
```

```python
import functools

import jax
import jax.numpy as jnp
from jax import lax
from jax.experimental import pallas as pl
from jax.experimental.pallas import tpu as pltpu
from jax.sharding import Mesh, PartitionSpec as P

STEPS = 2
CORES = 2
BLOCKS = 8
F32, BF16 = jnp.float32, jnp.bfloat16
VMEM_BYTES = 8 * 2**20


def dot(a, b):
    return jnp.dot(a, b, preferred_element_type=F32)


def dot_t(a, b):
    return lax.dot_general(a, b, (((1,), (1,)), ((), ())), preferred_element_type=F32)


def kernel_call(body, out_shape, n_in, scalars=0, far=0, scratch=()):
    vmem = pl.BlockSpec(memory_space=pltpu.VMEM)
    specs = [pl.BlockSpec(memory_space=pltpu.SMEM)] * scalars + [pl.BlockSpec(memory_space=pl.ANY)] * far
    single = not isinstance(out_shape, (list, tuple))
    return pl.pallas_call(
        body,
        out_shape=out_shape,
        in_specs=specs + [vmem] * n_in,
        out_specs=vmem if single else [vmem] * len(out_shape),
        scratch_shapes=scratch,
        compiler_params=pltpu.CompilerParams(vmem_limit_bytes=VMEM_BYTES),
    )


def store_partial(out, gate, up):
    n, two, units = out.shape
    out[:, : two // 2, :] = gate.astype(BF16).reshape(n, two // 2, units)
    out[:, two // 2 :, :] = up.astype(BF16).reshape(n, two // 2, units)


def copy_tokens(tokens, out):
    n, cores, lines, cols = out.shape
    half = tokens.shape[0] // cores
    values = tokens[...].astype(F32)
    for c in range(cores):
        block = jnp.concatenate(
            [
                values[c * half + j : c * half + j + 1, k * cols : (k + 1) * cols]
                for j in range(half)
                for k in range(lines // half)
            ],
            axis=0,
        ).astype(BF16)
        for h in range(n):
            out[h, c] = block


def first_products(
    place, gate_far, up_far, gathered, gate_there, up_there, out, block, stream, gate, up, sems
):
    fetches = [
        pltpu.make_async_copy(gate_far, gate, sems.at[0]),
        pltpu.make_async_copy(up_far, up, sems.at[1]),
    ]
    for fetch in fetches:
        fetch.start()
    n_hid, cores, lines, cols = gathered.shape
    n_blocks, rows, _ = stream.shape
    half, parts = rows // n_hid, n_blocks // cores
    owners = min(n_hid, 256 // lines)
    size = owners * lines
    line = lax.broadcasted_iota(jnp.int32, (size, size), 0)
    k, row = line // (owners * half), line % (owners * half)
    source = row // half * lines + row % half * parts + k
    order = (source == lax.broadcasted_iota(jnp.int32, (size, size), 1)).astype(F32).astype(BF16)
    for which in range(cores):
        core = place[0] if which == 0 else 1 - place[0]
        for group in range(n_hid // owners):
            piece = gathered[pl.ds(group * owners, owners), core].reshape(size, cols)
            sorted_piece = dot(order, piece).astype(BF16).reshape(parts, owners * half, cols)
            start = group * owners * half
            stream[which * parts : (which + 1) * parts, start : start + owners * half] = sorted_piece
    size = block.shape[0]
    block[...] = stream[place[2], pl.ds(pl.multiple_of(place[1] * size, size), size), :]
    x, y = (
        jnp.concatenate([stream[which * parts + k] for k in range(parts)], axis=1)
        for which in range(cores)
    )
    gate_sum, up_sum = dot_t(y, gate_there[...]), dot_t(y, up_there[...])
    fetches[0].wait()
    gate_sum += dot_t(x, gate[...])
    fetches[1].wait()
    up_sum += dot_t(x, up[...])
    store_partial(out, gate_sum, up_sum)


def block_products(blocks, gate, up, gate_there, up_there, out):
    n_rows, n_cols, rows, cols = blocks.shape
    x, y = (
        jnp.concatenate([blocks[:, k].reshape(n_rows * rows, cols) for k in part], axis=1)
        for part in (range(n_cols // 2), range(n_cols // 2, n_cols))
    )
    store_partial(
        out,
        dot_t(x, gate[...]) + dot_t(y, gate_there[...]),
        dot_t(x, up[...]) + dot_t(y, up_there[...]),
    )


def activation(parts, out):
    total = parts[0].astype(F32)
    for k in range(1, parts.shape[0]):
        total += parts[k].astype(F32)
    rows = total.shape[0] // 2
    gate, up = total[:rows], total[rows:]
    hidden = (gate / (1.0 + jnp.exp(-gate)) * up).astype(BF16)
    for k in range(out.shape[0]):
        out[k] = hidden


def down_blocks(there_far, hidden, down, out, down_there, sems):
    fetch = pltpu.make_async_copy(there_far, down_there, sems.at[0])
    fetch.start()
    n_rows, n_cols, rows, cols = out.shape
    x = hidden[...].reshape(n_rows * rows, hidden.shape[-1])
    for half, weight in enumerate((down, down_there)):
        if half == 1:
            fetch.wait()
        for k in range(n_cols // 2):
            value = dot(x, weight[:, k * cols : (k + 1) * cols])
            out[:, half * (n_cols // 2) + k] = value.astype(BF16).reshape(n_rows, rows, cols)


def add_branch(parts, block, out, copies):
    total = parts[0].astype(F32)
    for k in range(1, parts.shape[0]):
        total += parts[k].astype(F32)
    stream = (block[...].astype(F32) + total).astype(BF16)
    out[...] = stream
    for k in range(copies.shape[0]):
        copies[k] = stream


def last_down(place, hidden, down, block, out):
    n, rows, units = hidden.shape
    total, cols = n * rows, block.shape[1]

    def source(width):
        row = lax.broadcasted_iota(jnp.int32, (total, width), 0)
        group, inner = row & ~(CORES * rows - 1), row & (CORES * rows - 1)
        pair = CORES * (rows // BLOCKS)
        owner, within = inner // pair, inner % pair
        return group + within // (pair // CORES) * rows + owner * (pair // CORES) + within % (pair // CORES)

    order = source(total) == lax.broadcasted_iota(jnp.int32, (total, total), 1)
    x = dot(order.astype(F32).astype(BF16), hidden[...].reshape(total, units)).astype(BF16)
    own_rows = source(rows) == lax.broadcasted_iota(jnp.int32, (total, rows), 1) + place[0] * rows
    addend = dot(own_rows.astype(F32).astype(BF16), block[...])
    n_blocks, own = down.shape[1] // cols, out.shape[2] // (down.shape[1] // cols)
    values, rolled = [], []
    for k in range(n_blocks):
        value = dot(x, down[:, k * cols : (k + 1) * cols])
        value += jnp.where(place[1] == k, addend, 0.0)
        values.append(value.reshape(total // (2 * own), 2 * own, cols))
        rolled.append(pltpu.roll(values[-1], own, 1))
    upper = lax.broadcasted_iota(jnp.int32, values[0].shape, 1) < own
    for k in range(0, n_blocks, 2):
        lines = slice(k * own, (k + 2) * own)
        out[:, 0, lines] = jnp.where(upper, values[k], rolled[k + 1]).astype(BF16)
        out[:, 1, lines] = jnp.where(upper, rolled[k], values[k + 1]).astype(BF16)


def final_sum(parts, out):
    total = parts[0].astype(F32)
    for k in range(1, parts.shape[0]):
        total += parts[k].astype(F32)
    own, cols = out.shape[0], total.shape[1]
    for k in range(out.shape[1] // cols):
        out[:, k * cols : (k + 1) * cols] = total[k * own : (k + 1) * own].astype(BF16)


def exchange(parts, axes):
    return lax.all_to_all(parts, axes, 0, 0, tiled=True)


def per_device(tokens, gate, up, down):
    n_hid, n_z = lax.axis_size("hid"), lax.axis_size("z")
    own, span = tokens.shape
    units = gate.shape[1]
    half = own // CORES
    rows = n_hid * half
    chunk = rows // n_z
    block_rows, block_cols = rows // BLOCKS, CORES * span // BLOCKS
    core, hid = lax.axis_index("core"), lax.axis_index("hid")
    row_block, col_block = hid // BLOCKS, hid % BLOCKS
    in_own = col_block < BLOCKS // 2

    swap = functools.partial(lax.ppermute, axis_name="core", perm=[(0, 1), (1, 0)])
    gate, up = gate.T, up.T
    weights = (gate, up, swap(gate), swap(up))
    down_there = swap(down)

    lines = half * span // block_cols
    copies_shape = jax.ShapeDtypeStruct((n_hid, CORES, lines, block_cols), BF16)
    copies = kernel_call(copy_tokens, copies_shape, 1)(tokens)
    gathered = exchange(copies.reshape(n_hid * CORES, lines, block_cols), ("hid", "core"))
    partial_shape = jax.ShapeDtypeStruct((n_z, 2 * chunk, units), BF16)
    partial_value, block = kernel_call(
        first_products,
        [partial_shape, jax.ShapeDtypeStruct((block_rows, block_cols), BF16)],
        3,
        scalars=1,
        far=2,
        scratch=[
            pltpu.VMEM((BLOCKS, rows, block_cols), BF16),
            pltpu.VMEM(gate.shape, BF16),
            pltpu.VMEM(up.shape, BF16),
            pltpu.SemaphoreType.DMA((2,)),
        ],
    )(
        jnp.stack([core, row_block, col_block]).astype(jnp.int32),
        pltpu.with_memory_space_constraint(gate, pltpu.HBM),
        pltpu.with_memory_space_constraint(up, pltpu.HBM),
        gathered.reshape(copies_shape.shape),
        *weights[2:],
    )
    partial_value, down_there = lax.optimization_barrier((partial_value, down_there))
    for repeat in range(STEPS):
        last = repeat == STEPS - 1
        parts = exchange(partial_value, "z")
        n_copies = n_z * CORES if last else n_z
        hidden_shape = jax.ShapeDtypeStruct((n_copies, chunk, units), BF16)
        hidden = kernel_call(activation, hidden_shape, 1)(parts)
        hidden = exchange(hidden, ("z", "core") if last else "z")
        if last:
            break
        blocks_shape = jax.ShapeDtypeStruct((BLOCKS, BLOCKS, block_rows, block_cols), BF16)
        down_part = kernel_call(
            down_blocks,
            blocks_shape,
            2,
            far=1,
            scratch=[pltpu.VMEM(down.shape, BF16), pltpu.SemaphoreType.DMA((1,))],
        )(down_there, hidden, down)
        parts = exchange(down_part.reshape(n_hid, block_rows, block_cols), "hid")
        block, copies = kernel_call(
            add_branch,
            [
                jax.ShapeDtypeStruct((block_rows, block_cols), BF16),
                jax.ShapeDtypeStruct((n_hid, block_rows, block_cols), BF16),
            ],
            2,
        )(parts, block)
        blocks = exchange(copies, "hid").reshape(blocks_shape.shape)
        partial_value = kernel_call(block_products, partial_shape, 5)(blocks, *weights)

    block = jnp.where(in_own, block, swap(block))
    block_core = jnp.where(in_own, core, 1 - core)
    place = jnp.stack([row_block * CORES + block_core, col_block % (BLOCKS // 2)]).astype(jnp.int32)
    n_lines = own * span // block_cols
    branch_shape = jax.ShapeDtypeStruct((n_hid // 2, 2, n_lines, block_cols), BF16)
    branch = kernel_call(last_down, branch_shape, 3, scalars=1)(place, hidden, down, block)
    parts = exchange(branch.reshape(n_hid, n_lines, block_cols), "hid")
    return kernel_call(final_sum, jax.ShapeDtypeStruct((own, span), BF16), 1)(parts)


def solution(mesh):
    n_hid, n_wid = mesh.devices.shape
    fine = Mesh(mesh.devices.reshape(n_hid, n_wid // CORES, CORES), ("hid", "z", "core"))
    wid = ("z", "core")
    in_specs = (P("hid", wid), P(wid, "hid"), P(wid, "hid"), P("hid", wid))
    out_specs = P("hid", wid)
    return jax.shard_map(
        per_device, mesh=fine, in_specs=in_specs, out_specs=out_specs, check_vma=False
    )
```

```python
import functools

import jax
import jax.numpy as jnp
from jax import lax
from jax.experimental import pallas as pl
from jax.experimental.pallas import tpu as pltpu
from jax.sharding import Mesh, PartitionSpec as P

STEPS = 2
CORES = 2
BLOCKS = 8
F32, BF16 = jnp.float32, jnp.bfloat16
VMEM_BYTES = 8 * 2**20


def dot(a, b):
    return jnp.dot(a, b, preferred_element_type=F32)


def dot_t(a, b):
    return lax.dot_general(a, b, (((1,), (1,)), ((), ())), preferred_element_type=F32)


def kernel_call(body, out_shape, n_in, scalars=0, far=0, scratch=()):
    vmem = pl.BlockSpec(memory_space=pltpu.VMEM)
    specs = [pl.BlockSpec(memory_space=pltpu.SMEM)] * scalars + [pl.BlockSpec(memory_space=pl.ANY)] * far
    single = not isinstance(out_shape, (list, tuple))
    return pl.pallas_call(
        body,
        out_shape=out_shape,
        in_specs=specs + [vmem] * n_in,
        out_specs=vmem if single else [vmem] * len(out_shape),
        scratch_shapes=scratch,
        compiler_params=pltpu.CompilerParams(vmem_limit_bytes=VMEM_BYTES),
    )


def store_partial(out, gate, up):
    n, two, units = out.shape
    out[:, : two // 2, :] = gate.astype(BF16).reshape(n, two // 2, units)
    out[:, two // 2 :, :] = up.astype(BF16).reshape(n, two // 2, units)


def copy_tokens(tokens, out):
    n, cores, lines, cols = out.shape
    half = tokens.shape[0] // cores
    values = tokens[...].astype(F32)
    for c in range(cores):
        block = jnp.concatenate(
            [
                values[c * half + j : c * half + j + 1, k * cols : (k + 1) * cols]
                for j in range(half)
                for k in range(lines // half)
            ],
            axis=0,
        ).astype(BF16)
        for h in range(n):
            out[h, c] = block


def first_products(
    place, gate_far, up_far, gathered, gate_there, up_there, out, block, stream, gate, up, sems
):
    fetches = [
        pltpu.make_async_copy(gate_far, gate, sems.at[0]),
        pltpu.make_async_copy(up_far, up, sems.at[1]),
    ]
    for fetch in fetches:
        fetch.start()
    n_hid, cores, lines, cols = gathered.shape
    n_blocks, rows, _ = stream.shape
    half, parts = rows // n_hid, n_blocks // cores
    owners = min(n_hid, 256 // lines)
    size = owners * lines
    line = lax.broadcasted_iota(jnp.int32, (size, 1), 0)
    k, row = line // (owners * half), line % (owners * half)
    source = row // half * lines + row % half * parts + k
    order = (source == lax.broadcasted_iota(jnp.int32, (size, size), 1)).astype(F32).astype(BF16)
    for which in range(cores):
        core = place[0] if which == 0 else 1 - place[0]
        for group in range(n_hid // owners):
            piece = gathered[pl.ds(group * owners, owners), core].reshape(size, cols)
            sorted_piece = dot(order, piece).astype(BF16).reshape(parts, owners * half, cols)
            start = group * owners * half
            stream[which * parts : (which + 1) * parts, start : start + owners * half] = sorted_piece
    size = block.shape[0]
    block[...] = stream[place[2], pl.ds(pl.multiple_of(place[1] * size, size), size), :]
    x, y = (
        jnp.concatenate([stream[which * parts + k] for k in range(parts)], axis=1)
        for which in range(cores)
    )
    gate_sum, up_sum = dot_t(y, gate_there[...]), dot_t(y, up_there[...])
    fetches[0].wait()
    gate_sum += dot_t(x, gate[...])
    fetches[1].wait()
    up_sum += dot_t(x, up[...])
    store_partial(out, gate_sum, up_sum)


def block_products(blocks, gate, up, gate_there, up_there, out):
    n_rows, n_cols, rows, cols = blocks.shape
    x, y = (
        jnp.concatenate([blocks[:, k].reshape(n_rows * rows, cols) for k in part], axis=1)
        for part in (range(n_cols // 2), range(n_cols // 2, n_cols))
    )
    store_partial(
        out,
        dot_t(x, gate[...]) + dot_t(y, gate_there[...]),
        dot_t(x, up[...]) + dot_t(y, up_there[...]),
    )


def activation(parts, out):
    total = parts[0].astype(F32)
    for k in range(1, parts.shape[0]):
        total += parts[k].astype(F32)
    rows = total.shape[0] // 2
    gate, up = total[:rows], total[rows:]
    hidden = (gate / (1.0 + jnp.exp(-gate)) * up).astype(BF16)
    for k in range(out.shape[0]):
        out[k] = hidden


def down_blocks(there_far, hidden, down, out, down_there, sems):
    fetch = pltpu.make_async_copy(there_far, down_there, sems.at[0])
    fetch.start()
    n_rows, n_cols, rows, cols = out.shape
    x = hidden[...].reshape(n_rows * rows, hidden.shape[-1])
    for half, weight in enumerate((down, down_there)):
        if half == 1:
            fetch.wait()
        for k in range(n_cols // 2):
            value = dot(x, weight[:, k * cols : (k + 1) * cols])
            out[:, half * (n_cols // 2) + k] = value.astype(BF16).reshape(n_rows, rows, cols)


def add_branch(parts, block, out, copies):
    total = parts[0].astype(F32)
    for k in range(1, parts.shape[0]):
        total += parts[k].astype(F32)
    stream = (block[...].astype(F32) + total).astype(BF16)
    out[...] = stream
    for k in range(copies.shape[0]):
        copies[k] = stream


def last_down(place, hidden, down, block, out):
    n, rows, units = hidden.shape
    total, cols = n * rows, block.shape[1]

    row = lax.broadcasted_iota(jnp.int32, (total, 1), 0)
    pair = CORES * (rows // BLOCKS)
    inner, within, half = row % (CORES * rows), row % pair, pair // CORES
    source = row - inner + within // half * rows + inner // pair * half + within % half
    order = source == lax.broadcasted_iota(jnp.int32, (total, total), 1)
    x = dot(order.astype(F32).astype(BF16), hidden[...].reshape(total, units)).astype(BF16)
    own_rows = source == lax.broadcasted_iota(jnp.int32, (total, rows), 1) + place[0] * rows
    addend = dot(own_rows.astype(F32).astype(BF16), block[...])
    n_blocks, own = down.shape[1] // cols, out.shape[2] // (down.shape[1] // cols)
    values, rolled = [], []
    for k in range(n_blocks):
        value = dot(x, down[:, k * cols : (k + 1) * cols])
        value += jnp.where(place[1] == k, addend, 0.0)
        values.append(value.reshape(total // (2 * own), 2 * own, cols))
        rolled.append(pltpu.roll(values[-1], own, 1))
    upper = lax.broadcasted_iota(jnp.int32, values[0].shape, 1) < own
    for k in range(0, n_blocks, 2):
        lines = slice(k * own, (k + 2) * own)
        out[:, 0, lines] = jnp.where(upper, values[k], rolled[k + 1]).astype(BF16)
        out[:, 1, lines] = jnp.where(upper, rolled[k], values[k + 1]).astype(BF16)


def final_sum(parts, out):
    total = parts[0].astype(F32)
    for k in range(1, parts.shape[0]):
        total += parts[k].astype(F32)
    own, cols = out.shape[0], total.shape[1]
    for k in range(out.shape[1] // cols):
        out[:, k * cols : (k + 1) * cols] = total[k * own : (k + 1) * own].astype(BF16)


def exchange(parts, axes):
    return lax.all_to_all(parts, axes, 0, 0, tiled=True)


def per_device(tokens, gate, up, down):
    n_hid, n_z = lax.axis_size("hid"), lax.axis_size("z")
    own, span = tokens.shape
    units = gate.shape[1]
    half = own // CORES
    rows = n_hid * half
    chunk = rows // n_z
    block_rows, block_cols = rows // BLOCKS, CORES * span // BLOCKS
    core, hid = lax.axis_index("core"), lax.axis_index("hid")
    row_block, col_block = hid // BLOCKS, hid % BLOCKS
    in_own = col_block < BLOCKS // 2

    swap = functools.partial(lax.ppermute, axis_name="core", perm=[(0, 1), (1, 0)])
    gate, up = gate.T, up.T
    weights = (gate, up, swap(gate), swap(up))
    down_there = swap(down)

    lines = half * span // block_cols
    copies_shape = jax.ShapeDtypeStruct((n_hid, CORES, lines, block_cols), BF16)
    copies = kernel_call(copy_tokens, copies_shape, 1)(tokens)
    gathered = exchange(copies.reshape(n_hid * CORES, lines, block_cols), ("hid", "core"))
    partial_shape = jax.ShapeDtypeStruct((n_z, 2 * chunk, units), BF16)
    partial_value, block = kernel_call(
        first_products,
        [partial_shape, jax.ShapeDtypeStruct((block_rows, block_cols), BF16)],
        3,
        scalars=1,
        far=2,
        scratch=[
            pltpu.VMEM((BLOCKS, rows, block_cols), BF16),
            pltpu.VMEM(gate.shape, BF16),
            pltpu.VMEM(up.shape, BF16),
            pltpu.SemaphoreType.DMA((2,)),
        ],
    )(
        jnp.stack([core, row_block, col_block]).astype(jnp.int32),
        pltpu.with_memory_space_constraint(gate, pltpu.HBM),
        pltpu.with_memory_space_constraint(up, pltpu.HBM),
        gathered.reshape(copies_shape.shape),
        *weights[2:],
    )
    partial_value, down_there = lax.optimization_barrier((partial_value, down_there))
    for repeat in range(STEPS):
        last = repeat == STEPS - 1
        parts = exchange(partial_value, "z")
        n_copies = n_z * CORES if last else n_z
        hidden_shape = jax.ShapeDtypeStruct((n_copies, chunk, units), BF16)
        hidden = kernel_call(activation, hidden_shape, 1)(parts)
        hidden = exchange(hidden, ("z", "core") if last else "z")
        if last:
            break
        blocks_shape = jax.ShapeDtypeStruct((BLOCKS, BLOCKS, block_rows, block_cols), BF16)
        down_part = kernel_call(
            down_blocks,
            blocks_shape,
            2,
            far=1,
            scratch=[pltpu.VMEM(down.shape, BF16), pltpu.SemaphoreType.DMA((1,))],
        )(down_there, hidden, down)
        parts = exchange(down_part.reshape(n_hid, block_rows, block_cols), "hid")
        block, copies = kernel_call(
            add_branch,
            [
                jax.ShapeDtypeStruct((block_rows, block_cols), BF16),
                jax.ShapeDtypeStruct((n_hid, block_rows, block_cols), BF16),
            ],
            2,
        )(parts, block)
        blocks = exchange(copies, "hid").reshape(blocks_shape.shape)
        partial_value = kernel_call(block_products, partial_shape, 5)(blocks, *weights)

    block = jnp.where(in_own, block, swap(block))
    block_core = jnp.where(in_own, core, 1 - core)
    place = jnp.stack([row_block * CORES + block_core, col_block % (BLOCKS // 2)]).astype(jnp.int32)
    n_lines = own * span // block_cols
    branch_shape = jax.ShapeDtypeStruct((n_hid // 2, 2, n_lines, block_cols), BF16)
    branch = kernel_call(last_down, branch_shape, 3, scalars=1)(place, hidden, down, block)
    parts = exchange(branch.reshape(n_hid, n_lines, block_cols), "hid")
    return kernel_call(final_sum, jax.ShapeDtypeStruct((own, span), BF16), 1)(parts)


def solution(mesh):
    n_hid, n_wid = mesh.devices.shape
    fine = Mesh(mesh.devices.reshape(n_hid, n_wid // CORES, CORES), ("hid", "z", "core"))
    wid = ("z", "core")
    in_specs = (P("hid", wid), P(wid, "hid"), P(wid, "hid"), P("hid", wid))
    out_specs = P("hid", wid)
    return jax.shard_map(
        per_device, mesh=fine, in_specs=in_specs, out_specs=out_specs, check_vma=False
    )
```

```python
import functools

import jax
import jax.numpy as jnp
from jax import lax
from jax.experimental import pallas as pl
from jax.experimental.pallas import tpu as pltpu
from jax.sharding import Mesh, PartitionSpec as P

STEPS = 2
CORES = 2
BLOCKS = 8
F32, BF16 = jnp.float32, jnp.bfloat16
VMEM_BYTES = 8 * 2**20


def dot(a, b):
    return jnp.dot(a, b, preferred_element_type=F32)


def dot_t(a, b):
    return lax.dot_general(a, b, (((1,), (1,)), ((), ())), preferred_element_type=F32)


def kernel_call(body, out_shape, n_in, scalars=0, far=0, scratch=()):
    vmem = pl.BlockSpec(memory_space=pltpu.VMEM)
    specs = [pl.BlockSpec(memory_space=pltpu.SMEM)] * scalars + [pl.BlockSpec(memory_space=pl.ANY)] * far
    single = not isinstance(out_shape, (list, tuple))
    return pl.pallas_call(
        body,
        out_shape=out_shape,
        in_specs=specs + [vmem] * n_in,
        out_specs=vmem if single else [vmem] * len(out_shape),
        scratch_shapes=scratch,
        compiler_params=pltpu.CompilerParams(vmem_limit_bytes=VMEM_BYTES),
    )


def store_partial(out, gate, up):
    n, rows, width = out.shape
    units = width // 2
    out[:, :, :units] = gate.astype(BF16).reshape(n, rows, units)
    out[:, :, units:] = up.astype(BF16).reshape(n, rows, units)


def copy_tokens(tokens, out):
    n, cores, lines, cols = out.shape
    half = tokens.shape[0] // cores
    values = tokens[...].astype(F32)
    for c in range(cores):
        block = jnp.concatenate(
            [
                values[c * half + j : c * half + j + 1, k * cols : (k + 1) * cols]
                for j in range(half)
                for k in range(lines // half)
            ],
            axis=0,
        ).astype(BF16)
        for h in range(n):
            out[h, c] = block


def first_products(
    place, gate_far, up_far, gathered, gate_there, up_there, out, block, stream, gate, up, sems
):
    fetches = [
        pltpu.make_async_copy(gate_far, gate, sems.at[0]),
        pltpu.make_async_copy(up_far, up, sems.at[1]),
    ]
    for fetch in fetches:
        fetch.start()
    n_hid, cores, lines, cols = gathered.shape
    n_blocks, rows, _ = stream.shape
    half, parts = rows // n_hid, n_blocks // cores
    owners = min(n_hid, 256 // lines)
    size = owners * lines
    line = lax.broadcasted_iota(jnp.int32, (size, 1), 0)
    k, row = line // (owners * half), line % (owners * half)
    source = row // half * lines + row % half * parts + k
    order = (source == lax.broadcasted_iota(jnp.int32, (size, size), 1)).astype(F32).astype(BF16)
    for which in range(cores):
        core = place[0] if which == 0 else 1 - place[0]
        for group in range(n_hid // owners):
            piece = gathered[pl.ds(group * owners, owners), core].reshape(size, cols)
            sorted_piece = dot(order, piece).astype(BF16).reshape(parts, owners * half, cols)
            start = group * owners * half
            stream[which * parts : (which + 1) * parts, start : start + owners * half] = sorted_piece
    size = block.shape[0]
    block[...] = stream[place[2], pl.ds(pl.multiple_of(place[1] * size, size), size), :]
    x, y = (
        jnp.concatenate([stream[which * parts + k] for k in range(parts)], axis=1)
        for which in range(cores)
    )
    gate_sum, up_sum = dot_t(y, gate_there[...]), dot_t(y, up_there[...])
    fetches[0].wait()
    gate_sum += dot_t(x, gate[...])
    fetches[1].wait()
    up_sum += dot_t(x, up[...])
    store_partial(out, gate_sum, up_sum)


def block_products(blocks, gate, up, gate_there, up_there, out):
    n_rows, n_cols, rows, cols = blocks.shape
    x, y = (
        jnp.concatenate([blocks[:, k].reshape(n_rows * rows, cols) for k in part], axis=1)
        for part in (range(n_cols // 2), range(n_cols // 2, n_cols))
    )
    store_partial(
        out,
        dot_t(x, gate[...]) + dot_t(y, gate_there[...]),
        dot_t(x, up[...]) + dot_t(y, up_there[...]),
    )


def activation(parts, out):
    total = parts[0].astype(F32)
    for k in range(1, parts.shape[0]):
        total += parts[k].astype(F32)
    units = total.shape[1] // 2
    gate, up = total[:, :units], total[:, units:]
    hidden = (gate / (1.0 + jnp.exp(-gate)) * up).astype(BF16)
    for k in range(out.shape[0]):
        out[k] = hidden


def down_blocks(there_far, hidden, down, out, down_there, sems):
    fetch = pltpu.make_async_copy(there_far, down_there, sems.at[0])
    fetch.start()
    n_rows, n_cols, rows, cols = out.shape
    x = hidden[...].reshape(n_rows * rows, hidden.shape[-1])
    for half, weight in enumerate((down, down_there)):
        if half == 1:
            fetch.wait()
        for k in range(n_cols // 2):
            value = dot(x, weight[:, k * cols : (k + 1) * cols])
            out[:, half * (n_cols // 2) + k] = value.astype(BF16).reshape(n_rows, rows, cols)


def add_branch(parts, block, out, copies):
    total = parts[0].astype(F32)
    for k in range(1, parts.shape[0]):
        total += parts[k].astype(F32)
    stream = (block[...].astype(F32) + total).astype(BF16)
    out[...] = stream
    for k in range(copies.shape[0]):
        copies[k] = stream


def last_down(place, hidden, down, block, out):
    n, rows, units = hidden.shape
    total, cols = n * rows, block.shape[1]

    row = lax.broadcasted_iota(jnp.int32, (total, 1), 0)
    pair = CORES * (rows // BLOCKS)
    inner, within, half = row % (CORES * rows), row % pair, pair // CORES
    source = row - inner + within // half * rows + inner // pair * half + within % half
    order = source == lax.broadcasted_iota(jnp.int32, (total, total), 1)
    x = dot(order.astype(F32).astype(BF16), hidden[...].reshape(total, units)).astype(BF16)
    own_rows = source == lax.broadcasted_iota(jnp.int32, (total, rows), 1) + place[0] * rows
    addend = dot(own_rows.astype(F32).astype(BF16), block[...])
    n_blocks, own = down.shape[1] // cols, out.shape[2] // (down.shape[1] // cols)
    values, rolled = [], []
    for k in range(n_blocks):
        value = dot(x, down[:, k * cols : (k + 1) * cols])
        value += jnp.where(place[1] == k, addend, 0.0)
        values.append(value.reshape(total // (2 * own), 2 * own, cols))
        rolled.append(pltpu.roll(values[-1], own, 1))
    upper = lax.broadcasted_iota(jnp.int32, values[0].shape, 1) < own
    for k in range(0, n_blocks, 2):
        lines = slice(k * own, (k + 2) * own)
        out[:, 0, lines] = jnp.where(upper, values[k], rolled[k + 1]).astype(BF16)
        out[:, 1, lines] = jnp.where(upper, rolled[k], values[k + 1]).astype(BF16)


def final_sum(parts, out):
    total = parts[0].astype(F32)
    for k in range(1, parts.shape[0]):
        total += parts[k].astype(F32)
    own, cols = out.shape[0], total.shape[1]
    for k in range(out.shape[1] // cols):
        out[:, k * cols : (k + 1) * cols] = total[k * own : (k + 1) * own].astype(BF16)


def exchange(parts, axes):
    return lax.all_to_all(parts, axes, 0, 0, tiled=True)


def per_device(tokens, gate, up, down):
    n_hid, n_z = lax.axis_size("hid"), lax.axis_size("z")
    own, span = tokens.shape
    units = gate.shape[1]
    half = own // CORES
    rows = n_hid * half
    chunk = rows // n_z
    block_rows, block_cols = rows // BLOCKS, CORES * span // BLOCKS
    core, hid = lax.axis_index("core"), lax.axis_index("hid")
    row_block, col_block = hid // BLOCKS, hid % BLOCKS
    in_own = col_block < BLOCKS // 2

    swap = functools.partial(lax.ppermute, axis_name="core", perm=[(0, 1), (1, 0)])
    gate, up = gate.T, up.T
    weights = (gate, up, swap(gate), swap(up))
    down_there = swap(down)

    lines = half * span // block_cols
    copies_shape = jax.ShapeDtypeStruct((n_hid, CORES, lines, block_cols), BF16)
    copies = kernel_call(copy_tokens, copies_shape, 1)(tokens)
    gathered = exchange(copies.reshape(n_hid * CORES, lines, block_cols), ("hid", "core"))
    partial_shape = jax.ShapeDtypeStruct((n_z, chunk, 2 * units), BF16)
    partial_value, block = kernel_call(
        first_products,
        [partial_shape, jax.ShapeDtypeStruct((block_rows, block_cols), BF16)],
        3,
        scalars=1,
        far=2,
        scratch=[
            pltpu.VMEM((BLOCKS, rows, block_cols), BF16),
            pltpu.VMEM(gate.shape, BF16),
            pltpu.VMEM(up.shape, BF16),
            pltpu.SemaphoreType.DMA((2,)),
        ],
    )(
        jnp.stack([core, row_block, col_block]).astype(jnp.int32),
        pltpu.with_memory_space_constraint(gate, pltpu.HBM),
        pltpu.with_memory_space_constraint(up, pltpu.HBM),
        gathered.reshape(copies_shape.shape),
        *weights[2:],
    )
    partial_value, down_there = lax.optimization_barrier((partial_value, down_there))
    for repeat in range(STEPS):
        last = repeat == STEPS - 1
        parts = exchange(partial_value, "z")
        n_copies = n_z * CORES if last else n_z
        hidden_shape = jax.ShapeDtypeStruct((n_copies, chunk, units), BF16)
        hidden = kernel_call(activation, hidden_shape, 1)(parts)
        hidden = exchange(hidden, ("z", "core") if last else "z")
        if last:
            break
        blocks_shape = jax.ShapeDtypeStruct((BLOCKS, BLOCKS, block_rows, block_cols), BF16)
        down_part = kernel_call(
            down_blocks,
            blocks_shape,
            2,
            far=1,
            scratch=[pltpu.VMEM(down.shape, BF16), pltpu.SemaphoreType.DMA((1,))],
        )(down_there, hidden, down)
        parts = exchange(down_part.reshape(n_hid, block_rows, block_cols), "hid")
        block, copies = kernel_call(
            add_branch,
            [
                jax.ShapeDtypeStruct((block_rows, block_cols), BF16),
                jax.ShapeDtypeStruct((n_hid, block_rows, block_cols), BF16),
            ],
            2,
        )(parts, block)
        blocks = exchange(copies, "hid").reshape(blocks_shape.shape)
        partial_value = kernel_call(block_products, partial_shape, 5)(blocks, *weights)

    block = jnp.where(in_own, block, swap(block))
    block_core = jnp.where(in_own, core, 1 - core)
    place = jnp.stack([row_block * CORES + block_core, col_block % (BLOCKS // 2)]).astype(jnp.int32)
    n_lines = own * span // block_cols
    branch_shape = jax.ShapeDtypeStruct((n_hid // 2, 2, n_lines, block_cols), BF16)
    branch = kernel_call(last_down, branch_shape, 3, scalars=1)(place, hidden, down, block)
    parts = exchange(branch.reshape(n_hid, n_lines, block_cols), "hid")
    return kernel_call(final_sum, jax.ShapeDtypeStruct((own, span), BF16), 1)(parts)


def solution(mesh):
    n_hid, n_wid = mesh.devices.shape
    fine = Mesh(mesh.devices.reshape(n_hid, n_wid // CORES, CORES), ("hid", "z", "core"))
    wid = ("z", "core")
    in_specs = (P("hid", wid), P(wid, "hid"), P(wid, "hid"), P("hid", wid))
    out_specs = P("hid", wid)
    return jax.shard_map(
        per_device, mesh=fine, in_specs=in_specs, out_specs=out_specs, check_vma=False
    )
```
